32 devices in a mesh: groups: 2 (over y), out: 8 (over z, x), inp: 2 (over core).
Axes of the slice: x: 2, y: 2, z: 4, core: 2. Of those that a mesh axis runs over, the one named last changes fastest.
Arguments:
- attn: bfloat16 [32, 16384], P(('groups', 'out'), 'inp'), parts along dimension 0, may hold values from -6 to 6
- residual: bfloat16 [32, 16384], P(('groups', 'inp'), 'out'), parts along dimension 0, as said below
- out_weight: bfloat16 [16384, 16384], P('inp', 'out'), as said below
- norm_gain: bfloat16 [16384], P('out'), may hold values from 0.099609375 to 1.8984375
- query_weight: bfloat16 [16384, 16384], P('inp', 'out'), may hold values from -0.046875 to 0.046875
Outputs:
- stream: bfloat16 [32, 16384], P(('groups', 'inp'), 'out'), parts along dimension 0
- queries: bfloat16 [32, 16384], P(('groups', 'inp'), 'out'), parts along dimension 0
The draws below stay inside these ranges and needn't reach their ends.
There are 2 independent parts, one for each index of `groups`. The reference program is written for one: setup_inputs(seed, part) draws one part's arguments, and reference() takes and returns one part's arrays. A program takes and returns all parts, laid end to end along the dimension named above; an argument that names none is the same for every part. Nothing has to cross between parts.
Inputs may be any that keep to these rules, and one draw needn't show every extreme that they name: `residual`: its columns carry scales that differ widely. `out_weight`: entries of the output projection; columns carry scales that differ widely.
All inputs are finite; a program needn't handle non-finite values.
Results may differ from the reference program's by a relative error of at most 0.0057.
Values may be sent and summed in bfloat16 or wider, within the bound.
A program may use at most 192 MiB of HBM per device.

```python
import jax
import jax.numpy as jnp
from jax import lax

D = 16384
ROWS = 16
ATT = 16384


def column_scale(key, exponent):
    key = jax.random.fold_in(key, 7)
    where = jnp.arange(D, dtype=jnp.float32) / D
    jitter = jax.random.uniform(key, (D,), jnp.float32, -0.3, 0.3)
    return 10.0 ** (exponent * where - 1.0 + jitter)


def draw_residual(key, part):
    col_scale = column_scale(key, 2.0)
    key = jax.random.fold_in(key, 11)
    base_key, row_key = jax.random.split(key)
    row_scale = 10.0 ** jax.random.uniform(row_key, (ROWS, 1), jnp.float32, -0.5, 0.5)
    entries = jax.random.normal(base_key, (ROWS, D), jnp.float32)
    return (entries * row_scale * col_scale[None, :]).astype(jnp.bfloat16)


def draw_out_weight(key, part):
    col_scale = column_scale(key, 2.0)
    key = jax.random.fold_in(key, 13)
    entries = jax.random.normal(key, (ATT, D), jnp.float32)
    return (entries * ATT ** (-0.5) * col_scale[None, :]).astype(jnp.bfloat16)


def steps_of(key, shape, shards, least, largest):
    def one(position, blocks):
        heights = jax.random.uniform(jax.random.fold_in(jax.random.fold_in(key, 6), position), (blocks,), jnp.float32, least / len(shards), largest / len(shards))
        return jnp.repeat(jnp.exp(heights), shape[position] // blocks).reshape((-1,) + (1,) * (len(shape) - position - 1))

    factor_of = one(*shards[0])
    for cut in shards[1:]:
        factor_of = factor_of * one(*cut)
    return factor_of


def normal_values(rng, shape, spread, most, cuts=(), kind=jnp.bfloat16):
    array = jax.random.normal(rng, shape, jnp.float32) * spread
    if len(cuts) > 0:
        array = steps_of(rng, shape, cuts, -0.22, 0.18) * array
    return jnp.clip(array, min=-most, max=most).astype(kind)


def setup_inputs(seed: int = 0, part: int = 0) -> dict:
    key_of = jax.random.split(jax.random.key(seed), 6)
    own_keys = jax.random.split(jax.random.fold_in(key_of[5], part), 6)
    return {
        "attn": normal_values(own_keys[0], (ROWS, ATT), 1.0, 6.0, ((0, 8), (1, 2))),
        "residual": draw_residual(jax.random.fold_in(jax.random.fold_in(key_of[5], part), 71), part),
        "out_weight": draw_out_weight(jax.random.fold_in(key_of[5], 71), part),
        "norm_gain": jnp.clip(1.0 + 0.18 * jax.random.normal(key_of[3], (D,), jnp.float32), 0.099609375, 1.8984375).astype(jnp.bfloat16),
        "query_weight": normal_values(key_of[4], (D, ATT), D ** -0.5, 0.046875, ((0, 2), (1, 8))),
    }


def reference(attn, residual, out_weight, norm_gain, query_weight):
    projected = jnp.dot(attn, out_weight, preferred_element_type=jnp.float32)
    stream = (residual.astype(jnp.float32) + projected).astype(jnp.bfloat16)
    values = stream.astype(jnp.float32)
    mean_square = lax.optimization_barrier(jnp.sum(values * values, axis=1)) / D
    factor = lax.rsqrt(mean_square + 1e-05)
    normed = (values * factor[:, None] * norm_gain.astype(jnp.float32)[None, :]).astype(jnp.bfloat16)
    queries = jnp.dot(normed, query_weight, preferred_element_type=jnp.float32).astype(jnp.bfloat16)
    return (stream, queries)
```

```python
import functools

import jax
import jax.numpy as jnp
from jax import lax
from jax.experimental import pallas as pl
from jax.experimental.pallas import tpu as pltpu
from jax.sharding import PartitionSpec as P

epsilon = 1e-05
largest = 1e25
MESH = pl.DeviceIdType.MESH
f32, bf16 = jnp.float32, jnp.bfloat16


def wait_for(ref, sem):
    pltpu.make_async_copy(ref, ref, sem).wait()


def kernel(
    outs, attn, residual_hbm, gain_hbm, w1, w2, stream_o, query_o,
    residual, gain, land, lhs1, w1buf, w2buf, swap_send, swap_recv,
    gbuf, lhs2, ss_part, ss_land, acc, q_recv,
    small_sem, land_send, land_sem, w1_sem, w2_sem, swap_ssem, swap_rsem,
    g_send, g_recv, ss_send, ss_recv, q_ssem, q_rsem,
):
    o, i = lax.axis_index("out"), lax.axis_index("inp")
    half = outs // 2
    blocks, depth, width = w1buf.shape
    slots = w2buf.shape[0]
    rows = lhs1.shape[0]
    mine = rows // 2
    tiles, _, tile = acc.shape
    own = pl.ds(pl.multiple_of(i * mine, 8), mine)
    other = pl.ds(pl.multiple_of((1 - i) * mine, 8), mine)
    home = lax.div(o, half)
    place = lax.rem(o, half)

    barrier = pltpu.get_barrier_semaphore()
    me = o * 2 + i

    def greet(d, c):
        peer = lax.rem(me + d, 2 * outs)
        pl.semaphore_signal(
            barrier, inc=1,
            device_id={"out": lax.div(peer, 2), "inp": lax.rem(peer, 2)},
            device_id_type=MESH,
        )
        return c

    lax.fori_loop(1, 2 * outs, greet, 0)

    pltpu.make_async_copy(attn, land.at[o], land_sem.at[o]).start()
    pltpu.make_async_copy(residual_hbm, residual, small_sem.at[0]).start()
    pltpu.make_async_copy(gain_hbm, gain, small_sem.at[1]).start()

    def w1_copy(j):
        return pltpu.make_async_copy(
            w1.at[:, pl.ds(pl.multiple_of(j * width, 128), width)], w1buf.at[j], w1_sem.at[j]
        )

    full = half * width
    stride = blocks * width

    def w2_start(j):
        slot = lax.rem(j, slots)

        def piece(s, c):
            pltpu.make_async_copy(
                w2.at[pl.ds(pl.multiple_of(s * stride + j * width, 128), width)],
                w2buf.at[slot, pl.ds(pl.multiple_of(s * width, 128), width)],
                w2_sem.at[j, s],
            ).start()
            return c

        lax.fori_loop(0, half, piece, 0)

    for j in range(blocks):
        w1_copy(j).start()

    pl.semaphore_wait(barrier, 2 * outs - 1)

    def attn_copy(d):
        peer = lax.rem(o + d, outs)
        return pltpu.make_async_remote_copy(
            src_ref=attn, dst_ref=land.at[o], send_sem=land_send.at[d], recv_sem=land_sem.at[o],
            device_id={"out": peer}, device_id_type=MESH,
        )

    def loop(first, last, body):
        def step(d, c):
            body(d)
            return c

        lax.fori_loop(first, last, step, 0)

    loop(1, outs, lambda d: attn_copy(d).start())
    for j in range(slots):
        w2_start(j)

    each = land.shape[1]
    batch = 16 // each
    cut = min(1024, depth)

    def assemble(b):
        for t in range(batch):
            wait_for(land.at[b * batch + t], land_sem.at[b * batch + t])

        def columns(c):
            where = pl.ds(pl.multiple_of(c * cut, 128), cut)
            parts = [land[b * batch + t, :, where].astype(f32) for t in range(batch)]
            lhs1[pl.ds(pl.multiple_of(b * 16, 16), 16), where] = jnp.concatenate(
                parts, axis=0
            ).astype(bf16)

        loop(0, depth // cut, columns)

    loop(0, rows // 16, assemble)
    wait_for(residual, small_sem.at[0])
    wait_for(gain, small_sem.at[1])
    ss_part[...] = jnp.zeros_like(ss_part)

    def swap_copy(j):
        return pltpu.make_async_remote_copy(
            src_ref=swap_send.at[j], dst_ref=swap_recv.at[j],
            send_sem=swap_ssem.at[j], recv_sem=swap_rsem.at[j],
            device_id={"inp": 1 - i}, device_id_type=MESH,
        )

    def g_copy(j, t):
        peer = 2 * lax.rem(t + lax.div(o, 2), half) + i
        return pltpu.make_async_remote_copy(
            src_ref=gbuf.at[j],
            dst_ref=lhs2.at[j, :, pl.ds(pl.multiple_of(place * width, 128), width)],
            send_sem=g_send.at[j, t], recv_sem=g_recv.at[j, place],
            device_id={"out": peer, "inp": home}, device_id_type=MESH,
        )

    def g_local(j):
        return pltpu.make_async_copy(
            gbuf.at[j],
            lhs2.at[j, :, pl.ds(pl.multiple_of(place * width, 128), width)],
            g_recv.at[j, place],
        )

    def is_self(t):
        peer = 2 * lax.rem(t + lax.div(o, 2), half) + i
        return jnp.logical_and(peer == o, home == i)

    def post(j):
        where = pl.ds(pl.multiple_of(j * width, 128), width)
        swap_copy(j).wait_recv()
        summed = swap_send[j] + swap_recv[j]
        stream_o[:, where] = (swap_send[j, own, :] + swap_recv[j, own, :]).astype(bf16)
        values = summed.astype(bf16).astype(f32)
        scaled = values * gain[:, where].astype(f32)
        gbuf[j] = jnp.clip(scaled, -largest, largest).astype(bf16)

        def send(t):
            @pl.when(is_self(t))
            def _():
                g_local(j).start()

            @pl.when(jnp.logical_not(is_self(t)))
            def _():
                g_copy(j, t).start()

        loop(0, half, send)
        squares = values * values
        total = ss_part[...]
        for c in range(width // 128):
            total = total + squares[:, c * 128:(c + 1) * 128]
        ss_part[...] = total

    def project(j):
        w1_copy(j).wait()
        swap_send[j] = jnp.dot(lhs1[...], w1buf[j], preferred_element_type=f32)
        where = pl.ds(pl.multiple_of(j * width, 128), width)
        swap_send[j, own, :] += residual[:, where].astype(f32)
        swap_copy(j).start()

        @pl.when(j > 0)
        def _():
            post(j - 1)

    loop(0, blocks, project)
    post(blocks - 1)

    def ss_copy(d):
        peer = lax.rem(o + d, outs)
        return pltpu.make_async_remote_copy(
            src_ref=ss_part.at[own], dst_ref=ss_land.at[o],
            send_sem=ss_send.at[d], recv_sem=ss_recv.at[o],
            device_id={"out": peer}, device_id_type=MESH,
        )

    loop(1, outs, lambda d: ss_copy(d).start())
    ss_land[o] = ss_part[own, :]

    def q_copy(n):
        return pltpu.make_async_remote_copy(
            src_ref=acc.at[n, other], dst_ref=q_recv.at[n],
            send_sem=q_ssem.at[n], recv_sem=q_rsem.at[n],
            device_id={"inp": 1 - i}, device_id_type=MESH,
        )

    def query(j):
        slot = lax.rem(j, slots)

        def arrive(s):
            wait_for(
                lhs2.at[j, :, pl.ds(pl.multiple_of(s * width, 128), width)], g_recv.at[j, s]
            )
            wait_for(
                w2buf.at[slot, pl.ds(pl.multiple_of(s * width, 128), width)], w2_sem.at[j, s]
            )

        loop(0, half, arrive)

        def column(n):
            part = jnp.dot(
                lhs2[j],
                w2buf[slot, :, pl.ds(pl.multiple_of(n * tile, 128), tile)],
                preferred_element_type=f32,
            )

            @pl.when(j == 0)
            def _():
                acc[n] = part

            @pl.when(j > 0)
            def _():
                acc[n] += part

            @pl.when(j == blocks - 1)
            def _():
                q_copy(n).start()

        loop(0, tiles, column)
        if blocks > slots:
            @pl.when(j + slots < blocks)
            def _():
                w2_start(j + slots)

    loop(0, blocks, query)

    def ss_wait(d):
        s = lax.rem(o + d, outs)
        wait_for(ss_land.at[s], ss_recv.at[s])

    loop(1, outs, ss_wait)
    total = lax.fori_loop(
        0, outs, lambda s, t: t + ss_land[s], jnp.zeros((mine, 128), f32)
    )
    mean = jnp.sum(total, axis=1, keepdims=True) / (outs * stride)
    factor = lax.rsqrt(mean + epsilon)
    for n in range(tiles):
        q_copy(n).wait_recv()
        query_o[:, n * tile:(n + 1) * tile] = (
            (acc[n, own, :] + q_recv[n]) * factor
        ).astype(bf16)

    loop(1, outs, lambda d: attn_copy(d).wait_send())
    loop(1, outs, lambda d: ss_copy(d).wait_send())
    for n in range(tiles):
        q_copy(n).wait_send()

    def sent(j):
        swap_copy(j).wait_send()

        def one(t):
            @pl.when(jnp.logical_not(is_self(t)))
            def _():
                g_copy(j, t).wait_send()

        loop(0, half, one)

    loop(0, blocks, sent)


def on_device(outs, attn, residual, out_weight, norm_gain, query_weight):
    each, depth = attn.shape
    mine, features = residual.shape
    rows = 2 * mine
    half = outs // 2
    width = min(512, features)
    blocks = features // width
    slots = min(blocks, 3)
    tile = min(512, features)
    tiles = features // tile
    any_spec = pl.BlockSpec(memory_space=pl.ANY)
    vmem = pl.BlockSpec(memory_space=pltpu.VMEM)
    dma = pltpu.SemaphoreType.DMA
    return pl.pallas_call(
        functools.partial(kernel, outs),
        out_shape=[
            jax.ShapeDtypeStruct((mine, features), bf16),
            jax.ShapeDtypeStruct((mine, features), bf16),
        ],
        in_specs=[any_spec] * 5,
        out_specs=[vmem, vmem],
        scratch_shapes=[
            pltpu.VMEM((mine, features), bf16),
            pltpu.VMEM((1, features), bf16),
            pltpu.VMEM((outs, each, depth), bf16),
            pltpu.VMEM((rows, depth), bf16),
            pltpu.VMEM((blocks, depth, width), bf16),
            pltpu.VMEM((slots, half * width, features), bf16),
            pltpu.VMEM((blocks, rows, width), f32),
            pltpu.VMEM((blocks, rows, width), f32),
            pltpu.VMEM((blocks, rows, width), bf16),
            pltpu.VMEM((blocks, rows, half * width), bf16),
            pltpu.VMEM((rows, 128), f32),
            pltpu.VMEM((outs, mine, 128), f32),
            pltpu.VMEM((tiles, rows, tile), f32),
            pltpu.VMEM((tiles, mine, tile), f32),
            dma((2,)),
            dma((outs,)),
            dma((outs,)),
            dma((blocks,)),
            dma((blocks, half)),
            dma((blocks,)),
            dma((blocks,)),
            dma((blocks, half)),
            dma((blocks, half)),
            dma((outs,)),
            dma((outs,)),
            dma((tiles,)),
            dma((tiles,)),
        ],
        compiler_params=pltpu.CompilerParams(
            collective_id=0, has_side_effects=True, vmem_limit_bytes=62 * 1024 * 1024
        ),
        cost_estimate=pl.CostEstimate(
            flops=4 * rows * depth * features,
            bytes_accessed=4 * depth * features,
            transcendentals=0,
        ),
    )(attn, residual, norm_gain.reshape(1, features), out_weight, query_weight)


def solution(mesh):
    return jax.shard_map(
        functools.partial(on_device, mesh.shape["out"]),
        mesh=mesh,
        in_specs=(
            P(("groups", "out"), "inp"),
            P(("groups", "inp"), "out"),
            P("inp", "out"),
            P("out"),
            P("inp", "out"),
        ),
        out_specs=(P(("groups", "inp"), "out"), P(("groups", "inp"), "out")),
        check_vma=False,
    )
```

```python
import functools

import jax
import jax.numpy as jnp
from jax import lax
from jax.experimental import pallas as pl
from jax.experimental.pallas import tpu as pltpu
from jax.sharding import PartitionSpec as P

epsilon = 1e-05
largest = 1e25
MESH = pl.DeviceIdType.MESH
f32, bf16 = jnp.float32, jnp.bfloat16


def wait_for(ref, sem):
    pltpu.make_async_copy(ref, ref, sem).wait()


def kernel(
    outs, attn, residual_hbm, gain_hbm, w1, w2, both,
    residual, gain, gain32, land, lhs1, w1buf, w2buf, swap_send, swap_recv,
    gbuf, lhs2, ss_part, ss_land, acc, q_recv,
    small_sem, land_send, land_sem, w1_sem, w2_sem, swap_ssem, swap_rsem,
    g_send, g_recv, ss_send, ss_recv, q_ssem, q_rsem,
):
    o, i = lax.axis_index("out"), lax.axis_index("inp")
    half = outs // 2
    blocks, depth, width = w1buf.shape
    slots = w2buf.shape[0]
    rows = lhs1.shape[0]
    mine = rows // 2
    tiles, _, tile = acc.shape
    own = pl.ds(pl.multiple_of(i * mine, 8), mine)
    other = pl.ds(pl.multiple_of((1 - i) * mine, 8), mine)
    home = lax.div(o, half)
    place = lax.rem(o, half)

    barrier = pltpu.get_barrier_semaphore()
    me = o * 2 + i

    def greet(d, c):
        peer = lax.rem(me + d, 2 * outs)
        pl.semaphore_signal(
            barrier, inc=1,
            device_id={"out": lax.div(peer, 2), "inp": lax.rem(peer, 2)},
            device_id_type=MESH,
        )
        return c

    lax.fori_loop(1, 2 * outs, greet, 0)

    pltpu.make_async_copy(attn, land.at[o], land_sem.at[o]).start()
    pltpu.make_async_copy(residual_hbm, residual, small_sem.at[0]).start()
    pltpu.make_async_copy(gain_hbm, gain, small_sem.at[1]).start()

    def w1_copy(j):
        return pltpu.make_async_copy(
            w1.at[:, pl.ds(pl.multiple_of(j * width, 128), width)], w1buf.at[j], w1_sem.at[j]
        )

    full = half * width
    stride = blocks * width

    def w2_start(j):
        slot = lax.rem(j, slots)

        def piece(s, c):
            pltpu.make_async_copy(
                w2.at[pl.ds(pl.multiple_of(s * stride + j * width, 128), width)],
                w2buf.at[slot, pl.ds(pl.multiple_of(s * width, 128), width)],
                w2_sem.at[j, s],
            ).start()
            return c

        lax.fori_loop(0, half, piece, 0)

    for j in range(blocks):
        w1_copy(j).start()

    pl.semaphore_wait(barrier, 2 * outs - 1)

    def attn_copy(d):
        peer = lax.rem(o + d, outs)
        return pltpu.make_async_remote_copy(
            src_ref=attn, dst_ref=land.at[o], send_sem=land_send.at[d], recv_sem=land_sem.at[o],
            device_id={"out": peer}, device_id_type=MESH,
        )

    def loop(first, last, body):
        def step(d, c):
            body(d)
            return c

        lax.fori_loop(first, last, step, 0)

    loop(1, outs, lambda d: attn_copy(d).start())
    for j in range(slots):
        w2_start(j)

    each = land.shape[1]
    batch = 16 // each
    cut = min(1024, depth)

    def assemble(b):
        for t in range(batch):
            wait_for(land.at[b * batch + t], land_sem.at[b * batch + t])

        def columns(c):
            where = pl.ds(pl.multiple_of(c * cut, 128), cut)
            parts = [land[b * batch + t, :, where].astype(f32) for t in range(batch)]
            lhs1[pl.ds(pl.multiple_of(b * 16, 16), 16), where] = jnp.concatenate(
                parts, axis=0
            ).astype(bf16)

        loop(0, depth // cut, columns)

    loop(0, rows // 16, assemble)
    wait_for(residual, small_sem.at[0])
    wait_for(gain, small_sem.at[1])
    gain32[...] = gain[...].astype(f32)
    ss_part[...] = jnp.zeros_like(ss_part)

    def swap_copy(j):
        return pltpu.make_async_remote_copy(
            src_ref=swap_send.at[j], dst_ref=swap_recv.at[j],
            send_sem=swap_ssem.at[j], recv_sem=swap_rsem.at[j],
            device_id={"inp": 1 - i}, device_id_type=MESH,
        )

    def g_copy(j, t):
        peer = 2 * lax.rem(t + lax.div(o, 2), half) + i
        return pltpu.make_async_remote_copy(
            src_ref=gbuf.at[j],
            dst_ref=lhs2.at[j, :, pl.ds(pl.multiple_of(place * width, 128), width)],
            send_sem=g_send.at[j, t], recv_sem=g_recv.at[j, place],
            device_id={"out": peer, "inp": home}, device_id_type=MESH,
        )

    def g_local(j):
        return pltpu.make_async_copy(
            gbuf.at[j],
            lhs2.at[j, :, pl.ds(pl.multiple_of(place * width, 128), width)],
            g_recv.at[j, place],
        )

    def is_self(t):
        peer = 2 * lax.rem(t + lax.div(o, 2), half) + i
        return jnp.logical_and(peer == o, home == i)

    def post(j):
        where = pl.ds(pl.multiple_of(j * width, 128), width)
        swap_copy(j).wait_recv()
        summed = swap_send[j] + swap_recv[j]
        both[0, :, where] = (swap_send[j, own, :] + swap_recv[j, own, :]).astype(bf16)
        values = summed.astype(bf16).astype(f32)
        per = width // 128
        scaled = values * jnp.concatenate(
            [gain32[pl.ds(j * per + c, 1), :] for c in range(per)], axis=1
        )
        gbuf[j] = jnp.clip(scaled, -largest, largest).astype(bf16)

        def send(t):
            @pl.when(is_self(t))
            def _():
                g_local(j).start()

            @pl.when(jnp.logical_not(is_self(t)))
            def _():
                g_copy(j, t).start()

        loop(0, half, send)
        squares = values * values
        total = ss_part[...]
        for c in range(width // 128):
            total = total + squares[:, c * 128:(c + 1) * 128]
        ss_part[...] = total

    def project(j):
        w1_copy(j).wait()
        swap_send[j] = jnp.dot(lhs1[...], w1buf[j], preferred_element_type=f32)
        where = pl.ds(pl.multiple_of(j * width, 128), width)
        swap_send[j, own, :] += residual[:, where].astype(f32)
        swap_copy(j).start()

        @pl.when(j > 0)
        def _():
            post(j - 1)

    loop(0, blocks, project)
    post(blocks - 1)

    def ss_copy(d):
        peer = lax.rem(o + d, outs)
        return pltpu.make_async_remote_copy(
            src_ref=ss_part.at[own], dst_ref=ss_land.at[o],
            send_sem=ss_send.at[d], recv_sem=ss_recv.at[o],
            device_id={"out": peer}, device_id_type=MESH,
        )

    loop(1, outs, lambda d: ss_copy(d).start())
    ss_land[o] = ss_part[own, :]

    def q_copy(n):
        return pltpu.make_async_remote_copy(
            src_ref=acc.at[n, other], dst_ref=q_recv.at[n],
            send_sem=q_ssem.at[n], recv_sem=q_rsem.at[n],
            device_id={"inp": 1 - i}, device_id_type=MESH,
        )

    def query(j):
        slot = lax.rem(j, slots)

        def arrive(s):
            wait_for(
                lhs2.at[j, :, pl.ds(pl.multiple_of(s * width, 128), width)], g_recv.at[j, s]
            )
            wait_for(
                w2buf.at[slot, pl.ds(pl.multiple_of(s * width, 128), width)], w2_sem.at[j, s]
            )

        loop(0, half, arrive)

        def column(n):
            part = jnp.dot(
                lhs2[j],
                w2buf[slot, :, pl.ds(pl.multiple_of(n * tile, 128), tile)],
                preferred_element_type=f32,
            )

            @pl.when(j == 0)
            def _():
                acc[n] = part

            @pl.when(j > 0)
            def _():
                acc[n] += part

            @pl.when(j == blocks - 1)
            def _():
                q_copy(n).start()

        loop(0, tiles, column)
        if blocks > slots:
            @pl.when(j + slots < blocks)
            def _():
                w2_start(j + slots)

    loop(0, blocks, query)

    def ss_wait(d):
        s = lax.rem(o + d, outs)
        wait_for(ss_land.at[s], ss_recv.at[s])

    loop(1, outs, ss_wait)
    total = lax.fori_loop(
        0, outs, lambda s, t: t + ss_land[s], jnp.zeros((mine, 128), f32)
    )
    mean = jnp.sum(total, axis=1, keepdims=True) / (outs * stride)
    factor = lax.rsqrt(mean + epsilon)
    for n in range(tiles):
        q_copy(n).wait_recv()
        both[1, :, n * tile:(n + 1) * tile] = (
            (acc[n, own, :] + q_recv[n]) * factor
        ).astype(bf16)

    loop(1, outs, lambda d: attn_copy(d).wait_send())
    loop(1, outs, lambda d: ss_copy(d).wait_send())
    for n in range(tiles):
        q_copy(n).wait_send()

    def sent(j):
        swap_copy(j).wait_send()

        def one(t):
            @pl.when(jnp.logical_not(is_self(t)))
            def _():
                g_copy(j, t).wait_send()

        loop(0, half, one)

    loop(0, blocks, sent)


def on_device(outs, attn, residual, out_weight, norm_gain, query_weight):
    each, depth = attn.shape
    mine, features = residual.shape
    rows = 2 * mine
    half = outs // 2
    width = min(512, features)
    blocks = features // width
    slots = min(blocks, 3)
    tile = min(512, features)
    tiles = features // tile
    any_spec = pl.BlockSpec(memory_space=pl.ANY)
    vmem = pl.BlockSpec(memory_space=pltpu.VMEM)
    dma = pltpu.SemaphoreType.DMA
    results = pl.pallas_call(
        functools.partial(kernel, outs),
        out_shape=[jax.ShapeDtypeStruct((2, mine, features), bf16)],
        in_specs=[any_spec] * 5,
        out_specs=[vmem],
        scratch_shapes=[
            pltpu.VMEM((mine, features), bf16),
            pltpu.VMEM((features // 128, 128), bf16),
            pltpu.VMEM((features // 128, 128), f32),
            pltpu.VMEM((outs, each, depth), bf16),
            pltpu.VMEM((rows, depth), bf16),
            pltpu.VMEM((blocks, depth, width), bf16),
            pltpu.VMEM((slots, half * width, features), bf16),
            pltpu.VMEM((blocks, rows, width), f32),
            pltpu.VMEM((blocks, rows, width), f32),
            pltpu.VMEM((blocks, rows, width), bf16),
            pltpu.VMEM((blocks, rows, half * width), bf16),
            pltpu.VMEM((rows, 128), f32),
            pltpu.VMEM((outs, mine, 128), f32),
            pltpu.VMEM((tiles, rows, tile), f32),
            pltpu.VMEM((tiles, mine, tile), f32),
            dma((2,)),
            dma((outs,)),
            dma((outs,)),
            dma((blocks,)),
            dma((blocks, half)),
            dma((blocks,)),
            dma((blocks,)),
            dma((blocks, half)),
            dma((blocks, half)),
            dma((outs,)),
            dma((outs,)),
            dma((tiles,)),
            dma((tiles,)),
        ],
        compiler_params=pltpu.CompilerParams(
            collective_id=0, has_side_effects=True, vmem_limit_bytes=62 * 1024 * 1024
        ),
        cost_estimate=pl.CostEstimate(
            flops=4 * rows * depth * features,
            bytes_accessed=4 * depth * features,
            transcendentals=0,
        ),
    )(attn, residual, norm_gain.reshape(features // 128, 128), out_weight, query_weight)
    return results[0][0], results[0][1]


def solution(mesh):
    return jax.shard_map(
        functools.partial(on_device, mesh.shape["out"]),
        mesh=mesh,
        in_specs=(
            P(("groups", "out"), "inp"),
            P(("groups", "inp"), "out"),
            P("inp", "out"),
            P("out"),
            P("inp", "out"),
        ),
        out_specs=(P(("groups", "inp"), "out"), P(("groups", "inp"), "out")),
        check_vma=False,
    )
```

```python
import functools

import jax
import jax.numpy as jnp
from jax import lax
from jax.experimental import pallas as pl
from jax.experimental.pallas import tpu as pltpu
from jax.sharding import PartitionSpec as P

epsilon = 1e-05
largest = 1e25
MESH = pl.DeviceIdType.MESH
f32, bf16 = jnp.float32, jnp.bfloat16


def wait_for(ref, sem):
    pltpu.make_async_copy(ref, ref, sem).wait()


def kernel(
    outs, attn, residual_hbm, gain_hbm, w1, w2, both,
    residual, gain, gain32, land, lhs1, w1buf, w2buf, swap_send, swap_recv,
    gbuf, lhs2, ss_part, ss_land, acc, q_recv,
    small_sem, land_send, land_sem, w1_sem, w2_sem, swap_ssem, swap_rsem,
    g_send, g_recv, ss_send, ss_recv, q_ssem, q_rsem,
):
    o, i = lax.axis_index("out"), lax.axis_index("inp")
    half = outs // 2
    blocks, depth, width = w1buf.shape
    slots = w2buf.shape[0]
    rows = lhs1.shape[0]
    mine = rows // 2
    tiles, _, tile = acc.shape
    own = pl.ds(pl.multiple_of(i * mine, 8), mine)
    other = pl.ds(pl.multiple_of((1 - i) * mine, 8), mine)
    home = lax.div(o, half)
    place = lax.rem(o, half)

    barrier = pltpu.get_barrier_semaphore()
    me = o * 2 + i

    def greet(d, c):
        peer = lax.rem(me + d, 2 * outs)
        pl.semaphore_signal(
            barrier, inc=1,
            device_id={"out": lax.div(peer, 2), "inp": lax.rem(peer, 2)},
            device_id_type=MESH,
        )
        return c

    lax.fori_loop(1, 2 * outs, greet, 0, unroll=outs <= 8)

    pltpu.make_async_copy(attn, land.at[o], land_sem.at[o]).start()
    pltpu.make_async_copy(residual_hbm, residual, small_sem.at[0]).start()
    pltpu.make_async_copy(gain_hbm, gain, small_sem.at[1]).start()

    def w1_copy(j):
        return pltpu.make_async_copy(
            w1.at[:, pl.ds(pl.multiple_of(j * width, 128), width)], w1buf.at[j], w1_sem.at[j]
        )

    stride = blocks * width

    def w2_start(j):
        slot = lax.rem(j, slots)

        def piece(s, c):
            pltpu.make_async_copy(
                w2.at[pl.ds(pl.multiple_of(s * stride + j * width, 128), width)],
                w2buf.at[slot, pl.ds(pl.multiple_of(s * width, 128), width)],
                w2_sem.at[j, s],
            ).start()
            return c

        lax.fori_loop(0, half, piece, 0)

    for j in range(blocks):
        w1_copy(j).start()

    pl.semaphore_wait(barrier, 2 * outs - 1)

    def peer_of(d):
        near = lax.div(d - 1, half)
        block = near * home + (1 - near) * (1 - home)
        return block * half + lax.rem(place + d, half)

    def attn_copy(d):
        peer = peer_of(d)
        return pltpu.make_async_remote_copy(
            src_ref=attn, dst_ref=land.at[o], send_sem=land_send.at[d], recv_sem=land_sem.at[o],
            device_id={"out": peer}, device_id_type=MESH,
        )

    def loop(first, last, body):
        def step(d, c):
            body(d)
            return c

        lax.fori_loop(first, last, step, 0)

    loop(1, outs, lambda d: attn_copy(d).start())
    for j in range(slots):
        w2_start(j)

    each = land.shape[1]
    batch = 16 // each
    cut = min(1024, depth)

    def assemble(b):
        for t in range(batch):
            wait_for(land.at[b * batch + t], land_sem.at[b * batch + t])

        def columns(c):
            where = pl.ds(pl.multiple_of(c * cut, 128), cut)
            parts = [land[b * batch + t, :, where].astype(f32) for t in range(batch)]
            lhs1[pl.ds(pl.multiple_of(b * 16, 16), 16), where] = jnp.concatenate(
                parts, axis=0
            ).astype(bf16)

        loop(0, depth // cut, columns)

    loop(0, rows // 16, assemble)
    wait_for(residual, small_sem.at[0])
    wait_for(gain, small_sem.at[1])
    gain32[...] = gain[...].astype(f32)
    ss_part[...] = jnp.zeros_like(ss_part)

    def swap_copy(j):
        return pltpu.make_async_remote_copy(
            src_ref=swap_send.at[j], dst_ref=swap_recv.at[j],
            send_sem=swap_ssem.at[j], recv_sem=swap_rsem.at[j],
            device_id={"inp": 1 - i}, device_id_type=MESH,
        )

    def g_peer(t):
        quarter = half // 2
        near = lax.div(t, quarter)
        block = near * home + (1 - near) * (1 - home)
        return block * half + 2 * lax.rem(t + lax.div(place, 2), quarter) + i

    def g_copy(j, t):
        peer = g_peer(t)
        return pltpu.make_async_remote_copy(
            src_ref=gbuf.at[j],
            dst_ref=lhs2.at[j, :, pl.ds(pl.multiple_of(place * width, 128), width)],
            send_sem=g_send.at[j, t], recv_sem=g_recv.at[j, place],
            device_id={"out": peer, "inp": home}, device_id_type=MESH,
        )

    def g_local(j):
        return pltpu.make_async_copy(
            gbuf.at[j],
            lhs2.at[j, :, pl.ds(pl.multiple_of(place * width, 128), width)],
            g_recv.at[j, place],
        )

    def is_self(t):
        peer = g_peer(t)
        return jnp.logical_and(peer == o, home == i)

    def post(j):
        where = pl.ds(pl.multiple_of(j * width, 128), width)
        swap_copy(j).wait_recv()
        summed = swap_send[j] + swap_recv[j]
        both[0, :, where] = (swap_send[j, own, :] + swap_recv[j, own, :]).astype(bf16)
        values = summed.astype(bf16).astype(f32)
        per = width // 128
        scaled = values * jnp.concatenate(
            [gain32[pl.ds(j * per + c, 1), :] for c in range(per)], axis=1
        )
        gbuf[j] = jnp.clip(scaled, -largest, largest).astype(bf16)

        def send(t):
            @pl.when(is_self(t))
            def _():
                g_local(j).start()

            @pl.when(jnp.logical_not(is_self(t)))
            def _():
                g_copy(j, t).start()

        loop(0, half, send)
        squares = values * values
        total = ss_part[...]
        for c in range(width // 128):
            total = total + squares[:, c * 128:(c + 1) * 128]
        ss_part[...] = total

    def project(j):
        w1_copy(j).wait()
        swap_send[j] = jnp.dot(lhs1[...], w1buf[j], preferred_element_type=f32)
        where = pl.ds(pl.multiple_of(j * width, 128), width)
        swap_send[j, own, :] += residual[:, where].astype(f32)
        swap_copy(j).start()

        @pl.when(j > 0)
        def _():
            post(j - 1)

    loop(0, blocks, project)
    post(blocks - 1)

    def ss_copy(d):
        peer = lax.rem(o + d, outs)
        return pltpu.make_async_remote_copy(
            src_ref=ss_part.at[own], dst_ref=ss_land.at[o],
            send_sem=ss_send.at[d], recv_sem=ss_recv.at[o],
            device_id={"out": peer}, device_id_type=MESH,
        )

    loop(1, outs, lambda d: ss_copy(d).start())
    ss_land[o] = ss_part[own, :]

    def q_copy(n):
        return pltpu.make_async_remote_copy(
            src_ref=acc.at[n, other], dst_ref=q_recv.at[n],
            send_sem=q_ssem.at[n], recv_sem=q_rsem.at[n],
            device_id={"inp": 1 - i}, device_id_type=MESH,
        )

    def query(j):
        slot = lax.rem(j, slots)

        def arrive(s):
            wait_for(
                lhs2.at[j, :, pl.ds(pl.multiple_of(s * width, 128), width)], g_recv.at[j, s]
            )
            wait_for(
                w2buf.at[slot, pl.ds(pl.multiple_of(s * width, 128), width)], w2_sem.at[j, s]
            )

        loop(0, half, arrive)

        def column(n):
            part = jnp.dot(
                lhs2[j],
                w2buf[slot, :, pl.ds(pl.multiple_of(n * tile, 128), tile)],
                preferred_element_type=f32,
            )

            @pl.when(j == 0)
            def _():
                acc[n] = part

            @pl.when(j > 0)
            def _():
                acc[n] += part

            @pl.when(j == blocks - 1)
            def _():
                q_copy(n).start()

        loop(0, tiles, column)
        if blocks > slots:
            @pl.when(j + slots < blocks)
            def _():
                w2_start(j + slots)

    loop(0, blocks, query)

    def ss_wait(d):
        s = lax.rem(o + d, outs)
        wait_for(ss_land.at[s], ss_recv.at[s])

    loop(1, outs, ss_wait)
    total = lax.fori_loop(
        0, outs, lambda s, t: t + ss_land[s], jnp.zeros((mine, 128), f32)
    )
    mean = jnp.sum(total, axis=1, keepdims=True) / (outs * stride)
    factor = lax.rsqrt(mean + epsilon)
    for n in range(tiles):
        q_copy(n).wait_recv()
        both[1, :, n * tile:(n + 1) * tile] = (
            (acc[n, own, :] + q_recv[n]) * factor
        ).astype(bf16)

    loop(1, outs, lambda d: attn_copy(d).wait_send())
    loop(1, outs, lambda d: ss_copy(d).wait_send())
    for n in range(tiles):
        q_copy(n).wait_send()

    def sent(j):
        swap_copy(j).wait_send()

        def one(t):
            @pl.when(jnp.logical_not(is_self(t)))
            def _():
                g_copy(j, t).wait_send()

        loop(0, half, one)

    loop(0, blocks, sent)


def on_device(outs, attn, residual, out_weight, norm_gain, query_weight):
    each, depth = attn.shape
    mine, features = residual.shape
    rows = 2 * mine
    half = outs // 2
    width = min(512, features)
    blocks = features // width
    slots = min(blocks, 3)
    tile = min(512, features)
    tiles = features // tile
    any_spec = pl.BlockSpec(memory_space=pl.ANY)
    vmem = pl.BlockSpec(memory_space=pltpu.VMEM)
    dma = pltpu.SemaphoreType.DMA
    results = pl.pallas_call(
        functools.partial(kernel, outs),
        out_shape=[jax.ShapeDtypeStruct((2, mine, features), bf16)],
        in_specs=[any_spec] * 5,
        out_specs=[vmem],
        scratch_shapes=[
            pltpu.VMEM((mine, features), bf16),
            pltpu.VMEM((features // 128, 128), bf16),
            pltpu.VMEM((features // 128, 128), f32),
            pltpu.VMEM((outs, each, depth), bf16),
            pltpu.VMEM((rows, depth), bf16),
            pltpu.VMEM((blocks, depth, width), bf16),
            pltpu.VMEM((slots, half * width, features), bf16),
            pltpu.VMEM((blocks, rows, width), f32),
            pltpu.VMEM((blocks, rows, width), f32),
            pltpu.VMEM((blocks, rows, width), bf16),
            pltpu.VMEM((blocks, rows, half * width), bf16),
            pltpu.VMEM((rows, 128), f32),
            pltpu.VMEM((outs, mine, 128), f32),
            pltpu.VMEM((tiles, rows, tile), f32),
            pltpu.VMEM((tiles, mine, tile), f32),
            dma((2,)),
            dma((outs,)),
            dma((outs,)),
            dma((blocks,)),
            dma((blocks, half)),
            dma((blocks,)),
            dma((blocks,)),
            dma((blocks, half)),
            dma((blocks, half)),
            dma((outs,)),
            dma((outs,)),
            dma((tiles,)),
            dma((tiles,)),
        ],
        compiler_params=pltpu.CompilerParams(
            collective_id=0, has_side_effects=True, vmem_limit_bytes=62 * 1024 * 1024
        ),
        cost_estimate=pl.CostEstimate(
            flops=4 * rows * depth * features,
            bytes_accessed=4 * depth * features,
            transcendentals=0,
        ),
    )(attn, residual, norm_gain.reshape(features // 128, 128), out_weight, query_weight)
    return results[0][0], results[0][1]


def solution(mesh):
    return jax.shard_map(
        functools.partial(on_device, mesh.shape["out"]),
        mesh=mesh,
        in_specs=(
            P(("groups", "out"), "inp"),
            P(("groups", "inp"), "out"),
            P("inp", "out"),
            P("out"),
            P("inp", "out"),
        ),
        out_specs=(P(("groups", "inp"), "out"), P(("groups", "inp"), "out")),
        check_vma=False,
    )
```
